32 devices in a mesh: ctx: 16 (over z, y, core), fsdp: 2 (over x).
Axes of the slice: x: 2, y: 2, z: 4, core: 2. Of those that a mesh axis runs over, the one named last changes fastest.
Arguments:
- tokens: bfloat16 [4, 2048, 960], P('fsdp', 'ctx'), may hold values from -6 to 6
- cotangent: bfloat16 [4, 2048, 960], P('fsdp', 'ctx'), may hold values from -6 to 6
- early_block: int32 [4, 16], P('fsdp'), may hold values from 0 to 15, as said below
- positions: int32 [4, 2048], P('fsdp', 'ctx'), may hold values from 0 to 2047, as said below
- norm_gain: bfloat16 [960], P('fsdp'), may hold values from 0.5 to 1.5
- w_query: bfloat16 [960, 960], P('fsdp'), may hold values from -0.1875 to 0.1875
- w_key: bfloat16 [960, 320], P('fsdp'), may hold values from -0.1875 to 0.1875
- w_value: bfloat16 [960, 320], P('fsdp'), may hold values from -0.1875 to 0.1875
- w_out: bfloat16 [960, 960], P('fsdp'), may hold values from -1.5 to 1.5
- post_gain: bfloat16 [960], P('fsdp'), may hold values from 0.5 to 1.5
- w_gate: bfloat16 [960, 2560], P('fsdp'), may hold values from -0.1875 to 0.1875
- w_up: bfloat16 [960, 2560], P('fsdp'), may hold values from -0.1875 to 0.1875
- w_down: bfloat16 [2560, 960], P('fsdp'), may hold values from -0.125 to 0.125
Outputs:
- output: bfloat16 [4, 2048, 960], P('fsdp', 'ctx')
- grad_tokens: bfloat16 [4, 2048, 960], P('fsdp', 'ctx')
- grad_norm_gain: float32 [960], P('fsdp')
- grad_w_query: float32 [960, 960], P('fsdp')
- grad_w_key: float32 [960, 320], P('fsdp')
- grad_w_value: float32 [960, 320], P('fsdp')
- grad_w_out: float32 [960, 960], P('fsdp')
- grad_post_gain: float32 [960], P('fsdp')
- grad_w_gate: float32 [960, 2560], P('fsdp')
- grad_w_up: float32 [960, 2560], P('fsdp')
- grad_w_down: float32 [2560, 960], P('fsdp')
The draws below stay inside these ranges and needn't reach their ends.
Inputs may be any that keep to these rules, and one draw needn't show every extreme that they name: Each row is an ordering of 0 to 15; index c of ctx holds blocks early_block[s, c] and 31 - early_block[s, c] of sequence s. `positions`: in sequence order each sequence is a pack of documents; a token's position is its distance from its document's first token, and each sequence begins a document; the first sequence is a single document.
All inputs are finite; a program needn't handle non-finite values.
Results may differ from the reference program's by a relative error of at most 0.015.
Values may be sent and summed in bfloat16 or wider, within the bound.
A program may use at most 256 MiB of HBM per device.

```python
import math
import jax
import jax.numpy as jnp
from jax import lax

D = 960
H = 15
KVH = 5
HD = 64
FF = 2560
BLK = 64
SEQS = 4
SEQ_LEN = 2048
N_CTX = 16


def shared_blocks(key):
    base = jax.random.fold_in(key, 7)
    seq_keys = jax.random.split(base, SEQS)
    orders = jax.vmap(lambda one_key: jax.random.permutation(one_key, N_CTX))(seq_keys)
    return orders.astype(jnp.int32)


def draw_early_block(key, part):
    return shared_blocks(key)


def draw_positions(key, part):
    early = shared_blocks(key)
    length = 2 * N_CTX * BLK
    starts = jax.random.randint(jax.random.fold_in(key, 11), (SEQS, length), 0, 512) == 0
    index_row = jnp.arange(length, dtype=jnp.int32)[None, :]
    seq_column = jnp.arange(SEQS, dtype=jnp.int32)[:, None]
    starts = jnp.logical_and(starts, seq_column != 0)
    starts = jnp.logical_or(starts, index_row == 0)
    begins = lax.cummax(jnp.where(starts, index_row, 0), axis=1)
    in_document = (index_row - begins).astype(jnp.int32)
    blocks = jnp.stack([early, 2 * N_CTX - 1 - early], axis=-1)
    seq_index = (blocks[..., None] * BLK + jnp.arange(BLK, dtype=jnp.int32)).reshape(SEQS, length).astype(jnp.int32)
    return jnp.take_along_axis(in_document, seq_index, axis=1).astype(jnp.int32)


def shard_levels(rng, dims, cuts, low, largest):
    level, own = 1.0, jax.random.fold_in(rng, 6)
    for position, blocks in cuts:
        steps = jnp.exp(jax.random.uniform(jax.random.fold_in(own, position), (blocks,), jnp.float32, low / len(cuts), largest / len(cuts)))
        level = level * jnp.repeat(steps, dims[position] // blocks).reshape([-1 if axis == position else 1 for axis in range(len(dims))])
    return level


def centred(own_key, extent, width, bound, shards=(), held_as=jnp.bfloat16):
    result = width * jax.random.normal(own_key, extent, jnp.float32)
    if shards:
        result = result * shard_levels(own_key, extent, shards, -0.22, 0.18)
    return jnp.clip(result, -bound, bound).astype(held_as)


def setup_inputs(seed: int = 0) -> dict:
    key_list = jax.random.split(jax.random.key(seed), 14)
    tokens = centred(key_list[0], (SEQS, SEQ_LEN, D), 1.0, 6.0, ((0, 2), (1, 16)))
    cotangent = centred(key_list[1], (SEQS, SEQ_LEN, D), 1.0, 6.0, ((0, 2), (1, 16)))
    early_block = draw_early_block(jax.random.fold_in(key_list[13], 71), 0)
    positions = draw_positions(jax.random.fold_in(key_list[13], 71), 0)
    norm_gain = jnp.clip(1.0 + 0.1 * jax.random.normal(key_list[4], (D,), jnp.float32), 0.5, 1.5).astype(jnp.bfloat16)
    w_query = centred(key_list[5], (D, H * HD), D ** -0.5, 0.1875, ((0, 2),))
    w_key = centred(key_list[6], (D, KVH * HD), D ** -0.5, 0.1875, ((0, 2),))
    w_value = centred(key_list[7], (D, KVH * HD), D ** -0.5, 0.1875, ((0, 2),))
    w_out = centred(key_list[8], (H * HD, D), H ** -0.5, 1.5, ((0, 2),))
    post_gain = jnp.clip(1.0 + 0.1 * jax.random.normal(key_list[9], (D,), jnp.float32), 0.5, 1.5).astype(jnp.bfloat16)
    w_gate = centred(key_list[10], (D, FF), D ** -0.5, 0.1875, ((0, 2),))
    w_up = centred(key_list[11], (D, FF), D ** -0.5, 0.1875, ((0, 2),))
    w_down = centred(key_list[12], (FF, D), FF ** -0.5, 0.125, ((0, 2),))
    return {"tokens": tokens, "cotangent": cotangent, "early_block": early_block, "positions": positions, "norm_gain": norm_gain, "w_query": w_query, "w_key": w_key, "w_value": w_value, "w_out": w_out, "post_gain": post_gain, "w_gate": w_gate, "w_up": w_up, "w_down": w_down}


EPSILON = 1e-05
MASKED = -1e+30
PRECISE = lax.Precision.HIGHEST

@jax.custom_vjp
def low(v):
    return lax.optimization_barrier(v.astype(jnp.bfloat16)).astype(jnp.float32)

@jax.custom_vjp
def low_back(v):
    return v

def low_keep(v):
    return (low(v), None)

def low_pass(kept, grad):
    return (grad,)

def back_keep(v):
    return (v, None)

def back_low(kept, grad):
    return (low(grad),)
low.defvjp(low_keep, low_pass)
low_back.defvjp(back_keep, back_low)

def rope_tables(places, head_size):
    half_size = head_size // 2
    frequency = jnp.exp(jnp.arange(half_size, dtype=jnp.float32) * (-2.0 * math.log(10000.0) / head_size))
    angles = places.astype(jnp.float32)[..., None] * frequency
    return (jnp.cos(angles), jnp.sin(angles))

def rotate(values, cosines, sines):
    half_size = values.shape[-1] // 2
    first_half = values[..., :half_size]
    second_half = values[..., half_size:]
    return jnp.concatenate([first_half * cosines - second_half * sines, second_half * cosines + first_half * sines], axis=-1)

def rms_norm(values, gain):
    return values * lax.rsqrt(lax.optimization_barrier(jnp.mean(values * values, axis=-1, keepdims=True)) + EPSILON) * gain

def attend_sequence(entries):
    query_rows, key_rows, value_rows, places = entries
    length = query_rows.shape[0]
    stride = math.gcd(length, 512)
    number = length // stride
    factor = HD ** (-0.5)

    def one_block(block_entries):
        query_block, place_block = block_entries
        scores = low_back(jnp.einsum('qhgd,khd->hgqk', query_block, key_rows, precision=PRECISE) * factor)
        allowed = places[None, :] <= place_block[:, None]
        probability = low(jax.nn.softmax(jnp.where(allowed, scores, MASKED), axis=-1))
        return jnp.einsum('hgqk,khd->qhgd', probability, value_rows, precision=PRECISE)
    blocks_out = lax.map(jax.checkpoint(one_block), (query_rows.reshape((number, stride) + query_rows.shape[1:]), places.reshape(number, stride)))
    return blocks_out.reshape(query_rows.shape)

def layer(params, tokens_full, seq_places, cosines, sines):
    norm_gain, w_query, w_key, w_value, w_out, post_gain, w_gate, w_up, w_down = params
    seq_count, length, model_width = tokens_full.shape
    groups = H // KVH
    flat_rows = tokens_full.reshape(seq_count * length, model_width)
    normed = low(rms_norm(flat_rows, norm_gain))
    query_raw = low_back(jnp.dot(normed, w_query, precision=PRECISE)).reshape(seq_count, length, H, HD)
    key_raw = low_back(jnp.dot(normed, w_key, precision=PRECISE)).reshape(seq_count, length, KVH, HD)
    value_rows = low(low_back(jnp.dot(normed, w_value, precision=PRECISE))).reshape(seq_count, length, KVH, HD)
    query_rot = low(rotate(query_raw, cosines, sines)).reshape(seq_count, length, KVH, groups, HD)
    key_rot = low(rotate(key_raw, cosines, sines))
    attended = lax.map(attend_sequence, (query_rot, key_rot, value_rows, seq_places))
    mixed_rows = low(low_back(attended.reshape(seq_count * length, H * HD)))
    residual = flat_rows + low_back(jnp.dot(mixed_rows, w_out, precision=PRECISE))
    normed_two = low(rms_norm(residual, post_gain))
    gate_act = low_back(jnp.dot(normed_two, w_gate, precision=PRECISE))
    up_act = low_back(jnp.dot(normed_two, w_up, precision=PRECISE))
    hidden = low(jax.nn.silu(gate_act) * up_act)
    output = residual + low_back(jnp.dot(hidden, w_down, precision=PRECISE))
    return output.reshape(seq_count, length, model_width)

def reference(tokens, cotangent, early_block, positions, norm_gain, w_query, w_key, w_value, w_out, post_gain, w_gate, w_up, w_down):
    blocks = jnp.stack([early_block, 2 * N_CTX - 1 - early_block], axis=-1).astype(jnp.int32)
    seq_places = (blocks[..., None] * BLK + jnp.arange(BLK, dtype=jnp.int32)).reshape(SEQS, SEQ_LEN).astype(jnp.int32)
    cosines, sines = rope_tables(positions, HD)
    cosines = cosines[:, :, None, :]
    sines = sines[:, :, None, :]
    params = tuple((weight.astype(jnp.float32) for weight in (norm_gain, w_query, w_key, w_value, w_out, post_gain, w_gate, w_up, w_down)))

    def forward(param_list, tokens_full):
        return layer(param_list, tokens_full, seq_places, cosines, sines)
    output, pullback = jax.vjp(forward, params, tokens.astype(jnp.float32))
    grads, token_grad = pullback(cotangent.astype(jnp.float32))
    return (output.astype(jnp.bfloat16), token_grad.astype(jnp.bfloat16), grads[0], grads[1], grads[2], grads[3], grads[4], grads[5], grads[6], grads[7], grads[8])
```

```python
import math

import jax
import jax.numpy as jnp
from jax import lax
from jax.experimental import pallas as pl
from jax.experimental.pallas import tpu as pltpu
from jax.sharding import PartitionSpec as P

H = 15
KVH = 5
HD = 64


EPSILON = 1e-05
MASKED = -1e30


def rope_tables(places, head_size):
    half_size = head_size // 2
    frequency = jnp.exp(
        jnp.arange(half_size, dtype=jnp.float32) * (-2.0 * math.log(10000.0) / head_size)
    )
    angles = places.astype(jnp.float32)[..., None] * frequency
    return (jnp.cos(angles), jnp.sin(angles))


def rotate(values, cosines, sines):
    half = HD // 2
    width = values.shape[-1]
    ahead = jnp.concatenate([values[:, half:], values[:, :half]], axis=1)
    behind = jnp.concatenate([values[:, width - half :], values[:, : width - half]], axis=1)
    low = (jnp.arange(width, dtype=jnp.int32) % HD < half)[None, :]
    return values * cosines[:, :width] + jnp.where(low, -ahead, behind) * sines[:, :width]


def norm_scale(values):
    return lax.rsqrt(jnp.mean(values * values, axis=-1, keepdims=True) + EPSILON)


def norm_back(grad_normed, unit_rows, scale_rows, gain_row):
    weighted = grad_normed * gain_row
    return scale_rows * (
        weighted - unit_rows * jnp.mean(weighted * unit_rows, axis=-1, keepdims=True)
    )


def block_places(blocks, block_len):
    places = blocks[..., None] * block_len + jnp.arange(block_len, dtype=jnp.int32)
    return places.reshape(blocks.shape[:-1] + (2 * block_len,))


def swap_ctx(values, bit):
    number = lax.axis_size("ctx")
    return lax.ppermute(values, "ctx", [(i, i ^ (1 << bit)) for i in range(number)])


def swap_fsdp(values):
    return lax.ppermute(values, "fsdp", [(0, 1), (1, 0)])


def ctx_bit(bit):
    return (lax.axis_index("ctx") >> bit) & 1


def join(mine, other, bit, axis):
    first = jnp.where(bit == 0, mine, other)
    second = jnp.where(bit == 0, other, mine)
    return jnp.concatenate([first, second], axis=axis)


def gather_weight(part):
    rows = part.shape[0]
    quarter = rows // 4
    core, chip = ctx_bit(0), ctx_bit(1)
    piece = lax.dynamic_slice_in_dim(part, (core * 2 + chip) * quarter, quarter, 0)
    piece = swap_fsdp(piece)
    half = join(piece, swap_ctx(piece, 1), chip, 0)
    other = join(half, swap_ctx(half, 0), core, 0)
    return join(part, other, lax.axis_index("fsdp"), 0)


def half_of(values, bit, axis):
    size = values.shape[axis] // 2
    return lax.dynamic_slice_in_dim(values, bit * size, size, axis)


def reduce_grad(grad, lead):
    levels = lax.axis_size("ctx").bit_length() - 1
    order = list(lead) + [k for k in range(levels) if k not in lead]
    rows, columns = grad.shape
    total = grad.reshape(2, rows // 2, columns)
    steps = []
    for level in order:
        if level == "x":
            axis, bit = 0, lax.axis_index("fsdp")
        else:
            bit = ctx_bit(level)
            if total.shape[2] % 256 == 0 or total.shape[1] % 2:
                axis = 2
            else:
                axis = 1
            steps.append((level, bit, axis))
        sent = half_of(total, 1 - bit, axis).astype(jnp.bfloat16)
        arrived = swap_fsdp(sent) if level == "x" else swap_ctx(sent, level)
        total = half_of(total, bit, axis).astype(jnp.float32) + arrived.astype(jnp.float32)
    total = lax.reduce_precision(total, 8, 7).astype(jnp.bfloat16)
    for level, bit, axis in reversed(steps):
        total = join(total, swap_ctx(total, level), bit, axis)
    return total[0].astype(jnp.float32)


def scatter_rows(terms):
    devices = lax.axis_size("ctx")
    seqs, total_rows, width = terms.shape
    rows = total_rows // devices
    total = terms
    count = devices
    for level in range(devices.bit_length() - 1):
        bit = ctx_bit(level)
        count //= 2
        total = total.reshape(seqs, count, 2, rows, width)
        sent = lax.dynamic_index_in_dim(total, 1 - bit, 2, keepdims=False)
        kept = lax.dynamic_index_in_dim(total, bit, 2, keepdims=False)
        arrived = swap_ctx(sent.astype(jnp.bfloat16), level)
        total = kept.astype(jnp.float32) + arrived.astype(jnp.float32)
    return total.reshape(seqs * rows, width)


GROUPS = H // KVH
NT = (((1,), (1,)), ((), ()))
TN = (((0,), (0,)), ((), ()))
NN = (((1,), (0,)), ((), ()))


def dot(left, right, dims):
    return lax.dot_general(left, right, dims, preferred_element_type=jnp.float32)


def group_rows(ref, group):
    return jnp.concatenate(
        [ref[0, :, h * HD : (h + 1) * HD] for h in range(group * GROUPS, (group + 1) * GROUPS)],
        axis=0,
    )


def put_rows(ref, group, values):
    rows = values.shape[0] // GROUPS
    for g in range(GROUPS):
        h = group * GROUPS + g
        ref[0, :, h * HD : (h + 1) * HD] = values[g * rows : (g + 1) * rows]


def forward_kernel(q_ref, kv_ref, qp_ref, kp_ref, out_ref, lse_ref, max_s, sum_s, acc_s):
    step = pl.program_id(1)

    @pl.when(step == 0)
    def _():
        max_s[...] = jnp.full(max_s.shape, MASKED, jnp.float32)
        sum_s[...] = jnp.zeros(sum_s.shape, jnp.float32)
        acc_s[...] = jnp.zeros(acc_s.shape, jnp.float32)

    allowed = kp_ref[0] <= qp_ref[0]
    for j in range(KVH):
        query = group_rows(q_ref, j)
        key = kv_ref[0, :, j * HD : (j + 1) * HD]
        value = kv_ref[0, :, (KVH + j) * HD : (KVH + j + 1) * HD]
        scores = jnp.where(allowed, dot(key, query, NT), MASKED)
        top = jnp.maximum(max_s[j], jnp.max(scores, axis=0, keepdims=True))
        probs = jnp.exp(scores - top)
        scale = jnp.exp(max_s[j] - top)
        sum_s[j] = sum_s[j] * scale + jnp.sum(probs, axis=0, keepdims=True)
        acc_s[j] = acc_s[j] * scale + dot(value, probs.astype(jnp.bfloat16), TN)
        max_s[j] = top

    @pl.when(step == pl.num_programs(1) - 1)
    def _():
        for j in range(KVH):
            put_rows(out_ref, j, (acc_s[j] / sum_s[j]).T)
            lse_ref[0, j] = max_s[j] + jnp.log(sum_s[j])


def backward_kernel(
    q_ref, kv_ref, qp_ref, kp_ref, do_ref, out_ref, lse_ref, dq_ref, dkv_ref, dq_s
):
    step = pl.program_id(1)

    @pl.when(step == 0)
    def _():
        dq_s[...] = jnp.zeros(dq_s.shape, jnp.float32)

    allowed = kp_ref[0] <= qp_ref[0]
    for j in range(KVH):
        query = group_rows(q_ref, j)
        grad = group_rows(do_ref, j)
        key = kv_ref[0, :, j * HD : (j + 1) * HD]
        value = kv_ref[0, :, (KVH + j) * HD : (KVH + j + 1) * HD]
        product = grad.astype(jnp.float32) * group_rows(out_ref, j)
        delta = lax.dot_general(
            jnp.ones((8, HD), jnp.float32), product, NT,
            precision=lax.Precision.HIGHEST, preferred_element_type=jnp.float32,
        )[0:1]
        scores = jnp.where(allowed, dot(key, query, NT), MASKED)
        probs = jnp.exp(scores - lse_ref[0, j])
        grad_probs = dot(value, grad, NT)
        grad_scores = (probs * (grad_probs - delta)).astype(jnp.bfloat16)
        dq_s[j] += dot(key, grad_scores, TN)
        dkv_ref[0, :, j * HD : (j + 1) * HD] = dot(grad_scores, query, NN).astype(jnp.bfloat16)
        dkv_ref[0, :, (KVH + j) * HD : (KVH + j + 1) * HD] = dot(
            probs.astype(jnp.bfloat16), grad, NN
        ).astype(jnp.bfloat16)

    @pl.when(step == pl.num_programs(1) - 1)
    def _():
        for j in range(KVH):
            put_rows(dq_ref, j, (dq_s[j] * HD ** (-0.5)).T)


def attention_specs(seqs, rows, keys):
    chunk = min(keys, 2048)
    row = lambda width: pl.BlockSpec((1, rows, width), lambda s, c: (s, 0, 0))
    per_key = lambda width: pl.BlockSpec((1, chunk, width), lambda s, c: (s, c, 0))
    stat = pl.BlockSpec((1, KVH, 1, GROUPS * rows), lambda s, c: (s, 0, 0, 0))
    query_place = pl.BlockSpec((1, 1, GROUPS * rows), lambda s, c: (s, 0, 0))
    params = pltpu.CompilerParams(
        dimension_semantics=("arbitrary", "arbitrary"), vmem_limit_bytes=48 * 1024 * 1024
    )
    return (seqs, keys // chunk), row, per_key, stat, query_place, params


def attend_forward(query, key_value, query_places, key_places):
    seqs, rows, width = query.shape
    keys = key_value.shape[1]
    grid, row, per_key, stat, query_place, params = attention_specs(seqs, rows, keys)
    wide = GROUPS * rows
    return pl.pallas_call(
        forward_kernel,
        grid=grid,
        in_specs=[row(width), per_key(2 * KVH * HD), query_place, per_key(1)],
        out_specs=[row(width), stat],
        out_shape=[
            jax.ShapeDtypeStruct((seqs, rows, width), jnp.float32),
            jax.ShapeDtypeStruct((seqs, KVH, 1, wide), jnp.float32),
        ],
        scratch_shapes=[
            pltpu.VMEM((KVH, 1, wide), jnp.float32),
            pltpu.VMEM((KVH, 1, wide), jnp.float32),
            pltpu.VMEM((KVH, HD, wide), jnp.float32),
        ],
        cost_estimate=pl.CostEstimate(
            flops=seqs * H * rows * keys * 1000, bytes_accessed=2**23, transcendentals=0
        ),
        compiler_params=params,
        name="attend_forward",
    )(query, key_value, query_places, key_places)


def attend_backward(query, key_value, query_places, key_places, grad, out, log_total):
    seqs, rows, width = query.shape
    keys = key_value.shape[1]
    grid, row, per_key, stat, query_place, params = attention_specs(seqs, rows, keys)
    wide = GROUPS * rows
    both = 2 * KVH * HD
    return pl.pallas_call(
        backward_kernel,
        grid=grid,
        in_specs=[
            row(width), per_key(both), query_place, per_key(1), row(width), row(width), stat,
        ],
        out_specs=[row(width), per_key(both)],
        out_shape=[
            jax.ShapeDtypeStruct((seqs, rows, width), jnp.float32),
            jax.ShapeDtypeStruct((seqs, keys, both), jnp.bfloat16),
        ],
        scratch_shapes=[pltpu.VMEM((KVH, HD, wide), jnp.float32)],
        cost_estimate=pl.CostEstimate(
            flops=seqs * H * rows * keys * 2000, bytes_accessed=2**24, transcendentals=0
        ),
        compiler_params=params,
        name="attend_backward",
    )(query, key_value, query_places, key_places, grad, out, log_total)


def on_device(
    tokens,
    cotangent,
    early_block,
    positions,
    norm_gain,
    w_query,
    w_key,
    w_value,
    w_out,
    post_gain,
    w_gate,
    w_up,
    w_down,
):
    f32, bf16 = jnp.float32, jnp.bfloat16
    seq_count, rows_seq, model_width = tokens.shape
    block_len = rows_seq // 2
    devices = lax.axis_size("ctx")
    fsdp_place = lax.axis_index("fsdp")
    gains = jnp.stack([norm_gain, post_gain])
    gains = join(gains, swap_fsdp(gains), fsdp_place, 1).astype(f32)
    gain_one, gain_two = gains[0], gains[1]
    qkv_weight = gather_weight(jnp.concatenate([w_query, w_key, w_value], axis=1))
    out_weight = gather_weight(w_out)
    gate_weight = gather_weight(w_gate)
    up_weight = gather_weight(w_up)
    down_weight = gather_weight(w_down)

    flat_rows = tokens.reshape(-1, model_width).astype(f32)
    scale_one = norm_scale(flat_rows)
    unit_one = flat_rows * scale_one
    normed = (unit_one * gain_one).astype(bf16)
    qkv_raw = jnp.dot(normed, qkv_weight, preferred_element_type=f32)
    cosines, sines = rope_tables(positions.reshape(-1), HD)
    cosines = jnp.tile(cosines, (1, 2 * H))
    sines = jnp.tile(sines, (1, 2 * H))
    query_width, key_width = H * HD, KVH * HD
    key_rot = rotate(qkv_raw[:, query_width : query_width + key_width], cosines, sines)
    own_kv = jnp.concatenate(
        [key_rot.astype(bf16), qkv_raw[:, query_width + key_width :].astype(bf16)], axis=1
    ).reshape(seq_count, rows_seq, 2 * key_width)
    key_value = lax.all_gather(own_kv, "ctx", axis=1, tiled=True)
    query = (
        rotate(qkv_raw[:, :query_width], cosines, sines).astype(bf16) * bf16(HD ** (-0.5))
    ).reshape(seq_count, rows_seq, query_width)
    ctx_place = lax.axis_index("ctx")
    own_early = jnp.sum(
        jnp.where(jnp.arange(devices, dtype=jnp.int32)[None, :] == ctx_place, early_block, 0),
        axis=1,
    )
    own_places = block_places(
        jnp.stack([own_early, 2 * devices - 1 - own_early], axis=-1), block_len
    )
    all_places = block_places(
        jnp.stack([early_block, 2 * devices - 1 - early_block], axis=-1), block_len
    ).reshape(seq_count, devices * rows_seq, 1)
    query_places = jnp.tile(own_places, (1, GROUPS))[:, None, :]
    attended, log_total = attend_forward(query, key_value, query_places, all_places)
    mixed_rows = attended.reshape(-1, query_width).astype(bf16)
    residual = flat_rows + jnp.dot(mixed_rows, out_weight, preferred_element_type=f32)
    scale_two = norm_scale(residual)
    unit_two = residual * scale_two
    normed_two = (unit_two * gain_two).astype(bf16)
    gate_act = jnp.dot(normed_two, gate_weight, preferred_element_type=f32)
    up_act = jnp.dot(normed_two, up_weight, preferred_element_type=f32)
    sigmoid_gate = jax.nn.sigmoid(gate_act)
    hidden = (gate_act * sigmoid_gate * up_act).astype(bf16)
    output = (
        (residual + jnp.dot(hidden, down_weight, preferred_element_type=f32))
        .astype(bf16)
        .reshape(tokens.shape)
    )
    grad_out = cotangent.reshape(-1, model_width)
    grad_hidden = jnp.dot(grad_out, down_weight.T, preferred_element_type=f32)
    grad_up = (grad_hidden * gate_act * sigmoid_gate).astype(bf16)
    grad_gate = (
        grad_hidden * up_act * sigmoid_gate * (1.0 + gate_act * (1.0 - sigmoid_gate))
    ).astype(bf16)
    grad_normed_two = jnp.dot(grad_gate, gate_weight.T, preferred_element_type=f32) + jnp.dot(
        grad_up, up_weight.T, preferred_element_type=f32
    )
    grad_gain_two = jnp.sum(grad_normed_two * unit_two, axis=0)
    grad_residual = grad_out.astype(f32) + norm_back(
        grad_normed_two, unit_two, scale_two, gain_two
    )
    grad_residual_low = grad_residual.astype(bf16)
    grad_mixed = (
        jnp.dot(grad_residual_low, out_weight.T, preferred_element_type=f32)
        .astype(bf16)
        .reshape(seq_count, rows_seq, query_width)
    )
    grad_query, key_value_terms = attend_backward(
        query, key_value, query_places, all_places, grad_mixed, attended, log_total
    )
    owned_down = reduce_grad(
        jnp.dot(hidden.T, grad_out, preferred_element_type=f32).astype(bf16), (0, "x")
    )
    owned_gate = reduce_grad(
        jnp.dot(normed_two.T, grad_gate, preferred_element_type=f32).astype(bf16), (0, 1, "x")
    )
    owned_up = reduce_grad(
        jnp.dot(normed_two.T, grad_up, preferred_element_type=f32).astype(bf16), (0, 2, 1, "x")
    )
    owned_out = reduce_grad(
        jnp.dot(mixed_rows.T, grad_residual_low, preferred_element_type=f32).astype(bf16),
        (0, 2, "x"),
    )
    grad_kv = scatter_rows(key_value_terms)
    grad_qkv = jnp.concatenate(
        [
            rotate(grad_query.reshape(-1, query_width), cosines, -sines).astype(bf16),
            rotate(grad_kv[:, :key_width], cosines, -sines).astype(bf16),
            grad_kv[:, key_width:].astype(bf16),
        ],
        axis=1,
    )
    grad_qkv_w = jnp.dot(normed.T, grad_qkv, preferred_element_type=f32)
    grad_normed = jnp.dot(grad_qkv, qkv_weight.T, preferred_element_type=f32)
    grad_gain_one = jnp.sum(grad_normed * unit_one, axis=0)
    grad_input = (
        (grad_residual + norm_back(grad_normed, unit_one, scale_one, gain_one))
        .astype(bf16)
        .reshape(tokens.shape)
    )
    width = query_width + 2 * key_width
    tail = jnp.concatenate(
        [
            grad_qkv_w.astype(bf16),
            grad_gain_one.astype(bf16)[:, None],
            grad_gain_two.astype(bf16)[:, None],
            jnp.zeros((model_width, (-width - 2) % 128), bf16),
        ],
        axis=1,
    )
    tail = reduce_grad(tail, (0, "x"))
    return (
        output,
        grad_input,
        tail[:, width],
        tail[:, :query_width],
        tail[:, query_width : query_width + key_width],
        tail[:, query_width + key_width : width],
        owned_out,
        tail[:, width + 1],
        owned_gate,
        owned_up,
        owned_down,
    )


def solution(mesh):
    placed = (
        P("fsdp", "ctx", None),
        P("fsdp", "ctx", None),
        P("fsdp", None),
        P("fsdp", "ctx"),
        P("fsdp"),
        P("fsdp", None),
        P("fsdp", None),
        P("fsdp", None),
        P("fsdp", None),
        P("fsdp"),
        P("fsdp", None),
        P("fsdp", None),
        P("fsdp", None),
    )
    return jax.shard_map(
        on_device,
        mesh=mesh,
        in_specs=placed,
        out_specs=(
            P("fsdp", "ctx", None),
            P("fsdp", "ctx", None),
            P("fsdp"),
            P("fsdp", None),
            P("fsdp", None),
            P("fsdp", None),
            P("fsdp", None),
            P("fsdp"),
            P("fsdp", None),
            P("fsdp", None),
            P("fsdp", None),
        ),
        check_vma=False,
    )
```

```python
import math

import jax
import jax.numpy as jnp
from jax import lax
from jax.experimental import pallas as pl
from jax.experimental.pallas import tpu as pltpu
from jax.sharding import PartitionSpec as P

H = 15
KVH = 5
HD = 64


EPSILON = 1e-05
MASKED = -1e30


def rope_tables(places, head_size):
    half_size = head_size // 2
    frequency = jnp.exp(
        jnp.arange(half_size, dtype=jnp.float32) * (-2.0 * math.log(10000.0) / head_size)
    )
    angles = places.astype(jnp.float32)[..., None] * frequency
    return (jnp.cos(angles), jnp.sin(angles))


def rotate(values, cosines, sines):
    half = HD // 2
    width = values.shape[-1]
    ahead = jnp.concatenate([values[:, half:], values[:, :half]], axis=1)
    behind = jnp.concatenate([values[:, width - half :], values[:, : width - half]], axis=1)
    low = (jnp.arange(width, dtype=jnp.int32) % HD < half)[None, :]
    return values * cosines[:, :width] + jnp.where(low, -ahead, behind) * sines[:, :width]


def norm_scale(values):
    return lax.rsqrt(jnp.mean(values * values, axis=-1, keepdims=True) + EPSILON)


def norm_back(grad_normed, unit_rows, scale_rows, gain_row):
    weighted = grad_normed * gain_row
    return scale_rows * (
        weighted - unit_rows * jnp.mean(weighted * unit_rows, axis=-1, keepdims=True)
    )


def block_places(blocks, block_len):
    places = blocks[..., None] * block_len + jnp.arange(block_len, dtype=jnp.int32)
    return places.reshape(blocks.shape[:-1] + (2 * block_len,))


def swap_ctx(values, bit):
    number = lax.axis_size("ctx")
    return lax.ppermute(values, "ctx", [(i, i ^ (1 << bit)) for i in range(number)])


def swap_fsdp(values):
    return lax.ppermute(values, "fsdp", [(0, 1), (1, 0)])


def ctx_bit(bit):
    return (lax.axis_index("ctx") >> bit) & 1


def join(mine, other, bit, axis):
    first = jnp.where(bit == 0, mine, other)
    second = jnp.where(bit == 0, other, mine)
    return jnp.concatenate([first, second], axis=axis)


def fetch_quarter(part):
    rows = part.shape[0]
    quarter = rows // 4
    core, chip = ctx_bit(0), ctx_bit(1)
    piece = lax.dynamic_slice_in_dim(part, (core * 2 + chip) * quarter, quarter, 0)
    return swap_fsdp(piece)


def share_quarters(part, piece):
    core, chip = ctx_bit(0), ctx_bit(1)
    half = join(piece, swap_ctx(piece, 1), chip, 0)
    other = join(half, swap_ctx(half, 0), core, 0)
    return join(part, other, lax.axis_index("fsdp"), 0)


def after(*values):
    return lax.optimization_barrier(values)


def half_of(values, bit, axis):
    size = values.shape[axis] // 2
    return lax.dynamic_slice_in_dim(values, bit * size, size, axis)


def reduce_grad(grad, order):
    return gather_grad(*halve_grad(*halve_grad(grad, [], (0, "x")), order))


def halve_grad(total, steps, order):
    steps = list(steps)
    if total.ndim == 2:
        rows, columns = total.shape
        total = total.reshape(2, rows // 2, columns)
    for level in order:
        if level == "x":
            axis, bit = 0, lax.axis_index("fsdp")
        else:
            bit = ctx_bit(level)
            if total.shape[2] % 256 == 0 or total.shape[1] % 2:
                axis = 2
            else:
                axis = 1
            steps.append((level, bit, axis))
        sent = half_of(total, 1 - bit, axis).astype(jnp.bfloat16)
        arrived = swap_fsdp(sent) if level == "x" else swap_ctx(sent, level)
        total = half_of(total, bit, axis).astype(jnp.float32) + arrived.astype(jnp.float32)
    return total, steps


def gather_grad(total, steps):
    total = lax.reduce_precision(total, 8, 7).astype(jnp.bfloat16)
    for level, bit, axis in reversed(steps):
        total = join(total, swap_ctx(total, level), bit, axis)
    return total[0].astype(jnp.float32)


def scatter_rows(terms):
    devices = lax.axis_size("ctx")
    seqs, total_rows, width = terms.shape
    rows = total_rows // devices
    total = terms
    count = devices
    for level in range(devices.bit_length() - 1):
        bit = ctx_bit(level)
        count //= 2
        total = total.reshape(seqs, count, 2, rows, width)
        sent = lax.dynamic_index_in_dim(total, 1 - bit, 2, keepdims=False)
        kept = lax.dynamic_index_in_dim(total, bit, 2, keepdims=False)
        arrived = swap_ctx(sent.astype(jnp.bfloat16), level)
        total = kept.astype(jnp.float32) + arrived.astype(jnp.float32)
    return total.reshape(seqs * rows, width)


GROUPS = H // KVH
NT = (((1,), (1,)), ((), ()))
TN = (((0,), (0,)), ((), ()))
NN = (((1,), (0,)), ((), ()))


def dot(left, right, dims):
    return lax.dot_general(left, right, dims, preferred_element_type=jnp.float32)


def group_rows(ref, group):
    return jnp.concatenate(
        [ref[0, :, h * HD : (h + 1) * HD] for h in range(group * GROUPS, (group + 1) * GROUPS)],
        axis=0,
    )


def put_rows(ref, group, values):
    rows = values.shape[0] // GROUPS
    for g in range(GROUPS):
        h = group * GROUPS + g
        ref[0, :, h * HD : (h + 1) * HD] = values[g * rows : (g + 1) * rows]


def forward_kernel(q_ref, kv_ref, qp_ref, kp_ref, out_ref, lse_ref, max_s, sum_s, acc_s):
    step = pl.program_id(1)

    @pl.when(step == 0)
    def _():
        max_s[...] = jnp.full(max_s.shape, MASKED, jnp.float32)
        sum_s[...] = jnp.zeros(sum_s.shape, jnp.float32)
        acc_s[...] = jnp.zeros(acc_s.shape, jnp.float32)

    allowed = kp_ref[0] <= qp_ref[0]
    for j in range(KVH):
        query = group_rows(q_ref, j)
        key = kv_ref[0, :, j * HD : (j + 1) * HD]
        value = kv_ref[0, :, (KVH + j) * HD : (KVH + j + 1) * HD]
        scores = jnp.where(allowed, dot(key, query, NT), MASKED)
        top = jnp.maximum(max_s[j], jnp.max(scores, axis=0, keepdims=True))
        probs = jnp.exp(scores - top)
        scale = jnp.exp(max_s[j] - top)
        sum_s[j] = sum_s[j] * scale + jnp.sum(probs, axis=0, keepdims=True)
        acc_s[j] = acc_s[j] * scale + dot(value, probs.astype(jnp.bfloat16), TN)
        max_s[j] = top

    @pl.when(step == pl.num_programs(1) - 1)
    def _():
        for j in range(KVH):
            put_rows(out_ref, j, (acc_s[j] / sum_s[j]).T)
            lse_ref[0, j] = max_s[j] + jnp.log(sum_s[j])


def backward_kernel(
    q_ref, kv_ref, qp_ref, kp_ref, do_ref, out_ref, lse_ref, dq_ref, dkv_ref, dq_s
):
    step = pl.program_id(1)

    @pl.when(step == 0)
    def _():
        dq_s[...] = jnp.zeros(dq_s.shape, jnp.float32)

    allowed = kp_ref[0] <= qp_ref[0]
    for j in range(KVH):
        query = group_rows(q_ref, j)
        grad = group_rows(do_ref, j)
        key = kv_ref[0, :, j * HD : (j + 1) * HD]
        value = kv_ref[0, :, (KVH + j) * HD : (KVH + j + 1) * HD]
        product = grad.astype(jnp.float32) * group_rows(out_ref, j)
        delta = lax.dot_general(
            jnp.ones((8, HD), jnp.float32), product, NT,
            precision=lax.Precision.HIGHEST, preferred_element_type=jnp.float32,
        )[0:1]
        scores = jnp.where(allowed, dot(key, query, NT), MASKED)
        probs = jnp.exp(scores - lse_ref[0, j])
        grad_probs = dot(value, grad, NT)
        grad_scores = (probs * (grad_probs - delta)).astype(jnp.bfloat16)
        dq_s[j] += dot(key, grad_scores, TN)
        dkv_ref[0, :, j * HD : (j + 1) * HD] = dot(grad_scores, query, NN).astype(jnp.bfloat16)
        dkv_ref[0, :, (KVH + j) * HD : (KVH + j + 1) * HD] = dot(
            probs.astype(jnp.bfloat16), grad, NN
        ).astype(jnp.bfloat16)

    @pl.when(step == pl.num_programs(1) - 1)
    def _():
        for j in range(KVH):
            put_rows(dq_ref, j, (dq_s[j] * HD ** (-0.5)).T)


def attention_specs(seqs, rows, keys):
    chunk = min(keys, 2048)
    row = lambda width: pl.BlockSpec((1, rows, width), lambda s, c: (s, 0, 0))
    per_key = lambda width: pl.BlockSpec((1, chunk, width), lambda s, c: (s, c, 0))
    stat = pl.BlockSpec((1, KVH, 1, GROUPS * rows), lambda s, c: (s, 0, 0, 0))
    query_place = pl.BlockSpec((1, 1, GROUPS * rows), lambda s, c: (s, 0, 0))
    params = pltpu.CompilerParams(
        dimension_semantics=("arbitrary", "arbitrary"), vmem_limit_bytes=48 * 1024 * 1024
    )
    return (seqs, keys // chunk), row, per_key, stat, query_place, params


def attend_forward(query, key_value, query_places, key_places):
    seqs, rows, width = query.shape
    keys = key_value.shape[1]
    grid, row, per_key, stat, query_place, params = attention_specs(seqs, rows, keys)
    wide = GROUPS * rows
    return pl.pallas_call(
        forward_kernel,
        grid=grid,
        in_specs=[row(width), per_key(2 * KVH * HD), query_place, per_key(1)],
        out_specs=[row(width), stat],
        out_shape=[
            jax.ShapeDtypeStruct((seqs, rows, width), jnp.float32),
            jax.ShapeDtypeStruct((seqs, KVH, 1, wide), jnp.float32),
        ],
        scratch_shapes=[
            pltpu.VMEM((KVH, 1, wide), jnp.float32),
            pltpu.VMEM((KVH, 1, wide), jnp.float32),
            pltpu.VMEM((KVH, HD, wide), jnp.float32),
        ],
        cost_estimate=pl.CostEstimate(
            flops=seqs * H * rows * keys * 2600, bytes_accessed=2**23, transcendentals=0
        ),
        compiler_params=params,
        name="attend_forward",
    )(query, key_value, query_places, key_places)


def attend_backward(query, key_value, query_places, key_places, grad, out, log_total):
    seqs, rows, width = query.shape
    keys = key_value.shape[1]
    grid, row, per_key, stat, query_place, params = attention_specs(seqs, rows, keys)
    wide = GROUPS * rows
    both = 2 * KVH * HD
    return pl.pallas_call(
        backward_kernel,
        grid=grid,
        in_specs=[
            row(width), per_key(both), query_place, per_key(1), row(width), row(width), stat,
        ],
        out_specs=[row(width), per_key(both)],
        out_shape=[
            jax.ShapeDtypeStruct((seqs, rows, width), jnp.float32),
            jax.ShapeDtypeStruct((seqs, keys, both), jnp.bfloat16),
        ],
        scratch_shapes=[pltpu.VMEM((KVH, HD, wide), jnp.float32)],
        cost_estimate=pl.CostEstimate(
            flops=seqs * H * rows * keys * 4300, bytes_accessed=2**24, transcendentals=0
        ),
        compiler_params=params,
        name="attend_backward",
    )(query, key_value, query_places, key_places, grad, out, log_total)


def on_device(
    tokens,
    cotangent,
    early_block,
    positions,
    norm_gain,
    w_query,
    w_key,
    w_value,
    w_out,
    post_gain,
    w_gate,
    w_up,
    w_down,
):
    f32, bf16 = jnp.float32, jnp.bfloat16
    seq_count, rows_seq, model_width = tokens.shape
    block_len = rows_seq // 2
    devices = lax.axis_size("ctx")
    fsdp_place = lax.axis_index("fsdp")
    gains = jnp.stack([norm_gain, post_gain])
    gains = join(gains, swap_fsdp(gains), fsdp_place, 1).astype(f32)
    gain_one, gain_two = gains[0], gains[1]
    qkv_part = jnp.concatenate([w_query, w_key, w_value], axis=1)
    qkv_weight = share_quarters(qkv_part, fetch_quarter(qkv_part))
    out_weight = share_quarters(w_out, fetch_quarter(w_out))
    gate_piece, up_piece, down_piece = (fetch_quarter(w) for w in (w_gate, w_up, w_down))

    flat_rows = tokens.reshape(-1, model_width).astype(f32)
    scale_one = norm_scale(flat_rows)
    unit_one = flat_rows * scale_one
    normed = (unit_one * gain_one).astype(bf16)
    qkv_raw = jnp.dot(normed, qkv_weight, preferred_element_type=f32)
    cosines, sines = rope_tables(positions.reshape(-1), HD)
    cosines = jnp.tile(cosines, (1, 2 * H))
    sines = jnp.tile(sines, (1, 2 * H))
    query_width, key_width = H * HD, KVH * HD
    key_rot = rotate(qkv_raw[:, query_width : query_width + key_width], cosines, sines)
    own_kv = jnp.concatenate(
        [key_rot.astype(bf16), qkv_raw[:, query_width + key_width :].astype(bf16)], axis=1
    ).reshape(seq_count, rows_seq, 2 * key_width)
    key_value = lax.all_gather(own_kv, "ctx", axis=1, tiled=True)
    key_value, gate_piece, up_piece, down_piece = after(
        key_value, gate_piece, up_piece, down_piece
    )
    gate_weight = share_quarters(w_gate, gate_piece)
    up_weight = share_quarters(w_up, up_piece)
    down_weight = share_quarters(w_down, down_piece)
    query = (
        rotate(qkv_raw[:, :query_width], cosines, sines).astype(bf16) * bf16(HD ** (-0.5))
    ).reshape(seq_count, rows_seq, query_width)
    ctx_place = lax.axis_index("ctx")
    own_early = jnp.sum(
        jnp.where(jnp.arange(devices, dtype=jnp.int32)[None, :] == ctx_place, early_block, 0),
        axis=1,
    )
    own_places = block_places(
        jnp.stack([own_early, 2 * devices - 1 - own_early], axis=-1), block_len
    )
    all_places = block_places(
        jnp.stack([early_block, 2 * devices - 1 - early_block], axis=-1), block_len
    ).reshape(seq_count, devices * rows_seq, 1)
    query_places = jnp.tile(own_places, (1, GROUPS))[:, None, :]
    attended, log_total = attend_forward(query, key_value, query_places, all_places)
    mixed_rows = attended.reshape(-1, query_width).astype(bf16)
    residual = flat_rows + jnp.dot(mixed_rows, out_weight, preferred_element_type=f32)
    scale_two = norm_scale(residual)
    unit_two = residual * scale_two
    normed_two = (unit_two * gain_two).astype(bf16)
    gate_act = jnp.dot(normed_two, gate_weight, preferred_element_type=f32)
    up_act = jnp.dot(normed_two, up_weight, preferred_element_type=f32)
    sigmoid_gate = jax.nn.sigmoid(gate_act)
    hidden = (gate_act * sigmoid_gate * up_act).astype(bf16)
    output = (
        (residual + jnp.dot(hidden, down_weight, preferred_element_type=f32))
        .astype(bf16)
        .reshape(tokens.shape)
    )
    grad_out = cotangent.reshape(-1, model_width)
    grad_hidden = jnp.dot(grad_out, down_weight.T, preferred_element_type=f32)
    grad_up = (grad_hidden * gate_act * sigmoid_gate).astype(bf16)
    grad_gate = (
        grad_hidden * up_act * sigmoid_gate * (1.0 + gate_act * (1.0 - sigmoid_gate))
    ).astype(bf16)
    grad_normed_two = jnp.dot(grad_gate, gate_weight.T, preferred_element_type=f32) + jnp.dot(
        grad_up, up_weight.T, preferred_element_type=f32
    )
    grad_gain_two = jnp.sum(grad_normed_two * unit_two, axis=0)
    grad_residual = grad_out.astype(f32) + norm_back(
        grad_normed_two, unit_two, scale_two, gain_two
    )
    grad_residual_low = grad_residual.astype(bf16)
    grad_mixed = (
        jnp.dot(grad_residual_low, out_weight.T, preferred_element_type=f32)
        .astype(bf16)
        .reshape(seq_count, rows_seq, query_width)
    )
    down_sum, down_steps = halve_grad(
        jnp.dot(hidden.T, grad_out, preferred_element_type=f32).astype(bf16), [], (0,)
    )
    gate_sum, gate_steps = halve_grad(
        jnp.dot(normed_two.T, grad_gate, preferred_element_type=f32).astype(bf16), [], (0,)
    )
    grad_mixed, down_sum, gate_sum = after(grad_mixed, down_sum, gate_sum)
    query_terms, key_value_terms = [], []
    for sequence in range(seq_count):
        part = slice(sequence, sequence + 1)
        one_query, one_key_value = attend_backward(
            query[part], key_value[part], query_places[part], all_places[part],
            grad_mixed[part], attended[part], log_total[part],
        )
        query_terms.append(one_query)
        key_value_terms.append(one_key_value)
        if sequence == 0:
            down_sum, down_steps = halve_grad(down_sum, down_steps, ("x",))
            grad_mixed, down_sum = after(grad_mixed, down_sum)
    grad_query = jnp.concatenate(query_terms)
    key_value_terms = jnp.concatenate(key_value_terms)
    levels = range(1, lax.axis_size("ctx").bit_length() - 1)
    upward = tuple(levels)
    middle = (2, 1) + tuple(k for k in levels if k > 2)
    down_sum, down_steps = halve_grad(down_sum, down_steps, (1,))
    gate_sum, gate_steps = halve_grad(gate_sum, gate_steps, ("x",))
    up_sum, up_steps = halve_grad(
        jnp.dot(normed_two.T, grad_up, preferred_element_type=f32).astype(bf16), [], (0, "x")
    )
    out_sum, out_steps = halve_grad(
        jnp.dot(mixed_rows.T, grad_residual_low, preferred_element_type=f32).astype(bf16),
        [], (0, "x"),
    )
    grad_kv = scatter_rows(key_value_terms)
    grad_kv, down_sum, gate_sum, up_sum, out_sum = after(
        grad_kv, down_sum, gate_sum, up_sum, out_sum
    )
    owned_down = gather_grad(*halve_grad(down_sum, down_steps, upward[1:]))
    owned_gate = gather_grad(*halve_grad(gate_sum, gate_steps, middle))
    owned_up = gather_grad(*halve_grad(up_sum, up_steps, upward))
    owned_out = gather_grad(*halve_grad(out_sum, out_steps, middle))
    grad_qkv = jnp.concatenate(
        [
            rotate(grad_query.reshape(-1, query_width), cosines, -sines).astype(bf16),
            rotate(grad_kv[:, :key_width], cosines, -sines).astype(bf16),
            grad_kv[:, key_width:].astype(bf16),
        ],
        axis=1,
    )
    grad_qkv_w = jnp.dot(normed.T, grad_qkv, preferred_element_type=f32)
    grad_normed = jnp.dot(grad_qkv, qkv_weight.T, preferred_element_type=f32)
    grad_gain_one = jnp.sum(grad_normed * unit_one, axis=0)
    grad_input = (
        (grad_residual + norm_back(grad_normed, unit_one, scale_one, gain_one))
        .astype(bf16)
        .reshape(tokens.shape)
    )
    width = query_width + 2 * key_width
    tail = jnp.concatenate(
        [
            grad_qkv_w.astype(bf16),
            grad_gain_one.astype(bf16)[:, None],
            grad_gain_two.astype(bf16)[:, None],
            jnp.zeros((model_width, (-width - 2) % 128), bf16),
        ],
        axis=1,
    )
    tail = reduce_grad(tail, upward)
    return (
        output,
        grad_input,
        tail[:, width],
        tail[:, :query_width],
        tail[:, query_width : query_width + key_width],
        tail[:, query_width + key_width : width],
        owned_out,
        tail[:, width + 1],
        owned_gate,
        owned_up,
        owned_down,
    )


def solution(mesh):
    placed = (
        P("fsdp", "ctx", None),
        P("fsdp", "ctx", None),
        P("fsdp", None),
        P("fsdp", "ctx"),
        P("fsdp"),
        P("fsdp", None),
        P("fsdp", None),
        P("fsdp", None),
        P("fsdp", None),
        P("fsdp"),
        P("fsdp", None),
        P("fsdp", None),
        P("fsdp", None),
    )
    return jax.shard_map(
        on_device,
        mesh=mesh,
        in_specs=placed,
        out_specs=(
            P("fsdp", "ctx", None),
            P("fsdp", "ctx", None),
            P("fsdp"),
            P("fsdp", None),
            P("fsdp", None),
            P("fsdp", None),
            P("fsdp", None),
            P("fsdp"),
            P("fsdp", None),
            P("fsdp", None),
            P("fsdp", None),
        ),
        check_vma=False,
    )
```
